32 devices in a mesh: ctl: 4 (over z), seq: 8 (over y, x, core).
Axes of the slice: x: 2, y: 2, z: 4, core: 2. Of those that a mesh axis runs over, the one named last changes fastest.
Arguments:
- control_hidden_state: bfloat16 [8, 64, 48, 3072], P('seq', None, 'ctl'), may hold values from -60 to 60
- patch_segment_labels: int32 [8, 64, 48], P('seq', None, 'ctl'), may hold values from 0 to 149
- patch_depth_levels: int32 [8, 64, 48], P('seq', None, 'ctl'), may hold values from 0 to 255
- timestep: int32 [8], replicated, may hold values from 0 to 999
- segment_label_embedding: bfloat16 [150, 3072], replicated, may hold values from -3 to 3
- depth_level_embedding: bfloat16 [256, 3072], replicated, may hold values from -3 to 3
- timestep_weight: bfloat16 [256, 3072], replicated, may hold values from -0.875 to 0.875
- control_norm_gain: float32 [3072], replicated, may hold values from 0.1 to 1.9
- control_output_weight: bfloat16 [3072, 3072], P('ctl'), may hold values from -0.109375 to 0.109375
- transformer_hidden_state: bfloat16 [8, 64, 48, 3072], P('ctl', 'seq'), may hold values from -3 to 3
- query: bfloat16 [8, 64, 48, 2048], P('ctl', 'seq'), may hold values from -5 to 5
- key: bfloat16 [8, 64, 48, 2048], P('ctl', 'seq'), may hold values from -5 to 5
- value: bfloat16 [8, 64, 48, 2048], P('ctl', 'seq'), may hold values from -12 to 12
- attention_output_weight: bfloat16 [2048, 3072], P('ctl'), may hold values from -0.125 to 0.125
Outputs:
- next_hidden: bfloat16 [8, 64, 48, 3072], P('ctl', 'seq')
The draws below stay inside these ranges and needn't reach their ends.
All inputs are finite; a program needn't handle non-finite values.
Results may differ from the reference program's by a relative error of at most 0.0059.
Values may be sent and summed in bfloat16 or wider, within the bound.
A program may use at most 192 MiB of HBM per device.

```python
import math
import jax
import jax.numpy as jnp
from jax import lax

MODEL_WIDTH = 3072
HEADS = 16
HEAD_DIM = 128
SEG_CLASSES = 150
DEPTH_LEVELS = 256
FREQS = 256
STEPS_T = 1000
PATCH_ROWS = 64
PATCH_COLUMNS = 48
IMAGE_BATCH = 8
TOKENS = 3072
INNER = 2048


def drawn(key):
    base = jax.random.fold_in(key, 17)
    key_query, key_keys = jax.random.split(base, 2)
    array_shape = (IMAGE_BATCH, TOKENS, HEADS, HEAD_DIM)
    query_rows = jnp.clip(2.0 * jax.random.normal(key_query, array_shape, jnp.float32), -5.0, 5.0)
    keys_out = jnp.clip(jax.random.normal(key_keys, array_shape, jnp.float32), -5.0, 5.0)
    out_shape = (IMAGE_BATCH, PATCH_ROWS, PATCH_COLUMNS, HEADS * HEAD_DIM)
    return (query_rows.reshape(out_shape).astype(jnp.bfloat16), keys_out.reshape(out_shape).astype(jnp.bfloat16))


def draw_query(key, part):
    return drawn(key)[0]


def draw_key(key, part):
    return drawn(key)[1]


def draw_control_hidden_state(key, part):
    array_shape = (IMAGE_BATCH, PATCH_ROWS, PATCH_COLUMNS, MODEL_WIDTH)
    return jax.random.normal(key, array_shape, jnp.float32).astype(jnp.bfloat16)


def place_ends(result, rng, least, top_value):
    extent = result.shape
    spot = [jax.random.randint(jax.random.fold_in(rng, axis), (), 0, extent[axis]) for axis in range(len(extent))]
    result = result.at[tuple(spot)].set(least)
    longest = extent.index(max(extent))
    spot[longest] = (spot[longest] + 1) % extent[longest]
    return result.at[tuple(spot)].set(top_value)


def block_scale(rng, dims, cuts, least, top_value):
    def one(axis_at, shards_of):
        steps = jax.random.uniform(jax.random.fold_in(jax.random.fold_in(rng, 6), axis_at), (shards_of,), jnp.float32, least / len(cuts), top_value / len(cuts))
        return jnp.repeat(jnp.exp(steps), dims[axis_at] // shards_of).reshape((-1,) + (1,) * (len(dims) - axis_at - 1))

    level = one(*cuts[0])
    for cut in cuts[1:]:
        level = level * one(*cut)
    return level


def bell_draw(rng, extent, scale, bound, shards=(), held_as=jnp.bfloat16):
    drawn = scale * jax.random.normal(rng, extent, jnp.float32)
    if shards:
        drawn = drawn * block_scale(rng, extent, shards, -0.22, 0.18)
    return jnp.clip(drawn, -bound, bound).astype(held_as)


def setup_inputs(seed: int = 0) -> dict:
    key_list = jax.random.split(jax.random.key(seed), 15)
    return {
        "control_hidden_state": draw_control_hidden_state(jax.random.fold_in(key_list[14], 71), 0),
        "patch_segment_labels": place_ends(jax.random.randint(key_list[1], (IMAGE_BATCH, PATCH_ROWS, PATCH_COLUMNS), 0, SEG_CLASSES), jax.random.fold_in(key_list[1], 1), 0, SEG_CLASSES - 1).astype(jnp.int32),
        "patch_depth_levels": place_ends(jax.random.randint(key_list[2], (IMAGE_BATCH, PATCH_ROWS, PATCH_COLUMNS), 0, DEPTH_LEVELS), jax.random.fold_in(key_list[2], 1), 0, DEPTH_LEVELS - 1).astype(jnp.int32),
        "timestep": place_ends(jax.random.randint(key_list[3], (IMAGE_BATCH,), 0, STEPS_T), jax.random.fold_in(key_list[3], 1), 0, STEPS_T - 1).astype(jnp.int32),
        "segment_label_embedding": bell_draw(key_list[4], (SEG_CLASSES, MODEL_WIDTH), 0.5, 3.0),
        "depth_level_embedding": bell_draw(key_list[5], (DEPTH_LEVELS, MODEL_WIDTH), 0.5, 3.0),
        "timestep_weight": bell_draw(key_list[6], (FREQS, MODEL_WIDTH), 0.15, 0.875),
        "control_norm_gain": jnp.clip(1.0 + 0.18 * jax.random.normal(key_list[7], (MODEL_WIDTH,), jnp.float32), 0.1, 1.9),
        "control_output_weight": bell_draw(key_list[8], (MODEL_WIDTH, MODEL_WIDTH), MODEL_WIDTH ** -0.5, 0.109375, ((0, 4),)),
        "transformer_hidden_state": bell_draw(key_list[9], (IMAGE_BATCH, PATCH_ROWS, PATCH_COLUMNS, MODEL_WIDTH), 0.5, 3.0, ((0, 4), (1, 8))),
        "query": draw_query(jax.random.fold_in(key_list[14], 71), 0),
        "key": draw_key(jax.random.fold_in(key_list[14], 71), 0),
        "value": bell_draw(key_list[12], (IMAGE_BATCH, PATCH_ROWS, PATCH_COLUMNS, INNER), 2.0, 12.0, ((0, 4), (1, 8))),
        "attention_output_weight": bell_draw(key_list[13], (INNER, MODEL_WIDTH), INNER ** -0.5, 0.125, ((0, 4),)),
    }


def time_embed(timestep, timestep_weight):
    half = FREQS // 2
    freqs = jnp.exp(-math.log(10000.0) * jnp.arange(half, dtype=jnp.float32) / half)
    angles = timestep.astype(jnp.float32)[:, None] * freqs[None, :]
    features = jnp.concatenate([jnp.cos(angles), jnp.sin(angles)], axis=1).astype(jnp.bfloat16)
    return jax.nn.silu(jnp.dot(features, timestep_weight, preferred_element_type=jnp.float32))

def attend_head(entry_list):
    query_rows, input_keys, value_rows = entry_list
    scores = jnp.dot(query_rows, input_keys.T, preferred_element_type=jnp.float32) * HEAD_DIM ** (-0.5)
    peak = lax.optimization_barrier(jnp.max(scores, axis=1, keepdims=True))
    weights = jnp.exp(scores - peak)
    totals = lax.optimization_barrier(jnp.sum(weights, axis=1, keepdims=True))
    mixed = jnp.dot(weights.astype(jnp.bfloat16), value_rows, preferred_element_type=jnp.float32) / totals
    return mixed.astype(jnp.bfloat16)

def per_head(array):
    return jnp.transpose(array.reshape(TOKENS, HEADS, HEAD_DIM), (1, 0, 2))

def reference(control_hidden_state, patch_segment_labels, patch_depth_levels, timestep, segment_label_embedding, depth_level_embedding, timestep_weight, control_norm_gain, control_output_weight, transformer_hidden_state, query, key, value, attention_output_weight):
    timestep_gain = time_embed(timestep, timestep_weight)

    def single_image(entry_list):
        hidden_state, segment_vectors, depth_vectors, gain_vector, transformer_rows, query_rows, input_keys, value_rows = entry_list
        mixed = hidden_state.reshape(-1, MODEL_WIDTH).astype(jnp.float32) + segment_label_embedding[segment_vectors.reshape(-1)].astype(jnp.float32) + depth_level_embedding[depth_vectors.reshape(-1)].astype(jnp.float32)
        scale = lax.rsqrt(lax.optimization_barrier(jnp.mean(mixed * mixed, axis=-1, keepdims=True)) + 1e-06)
        normed = (mixed * scale * control_norm_gain * (1.0 + gain_vector)).astype(jnp.bfloat16)
        control_residual = jnp.dot(normed, control_output_weight, preferred_element_type=jnp.float32).astype(jnp.bfloat16)
        attended = lax.map(attend_head, (per_head(query_rows), per_head(input_keys), per_head(value_rows)))
        joined = jnp.transpose(attended, (1, 0, 2)).reshape(TOKENS, HEADS * HEAD_DIM)
        projected_rows = jnp.dot(joined, attention_output_weight, preferred_element_type=jnp.float32)
        final_output = transformer_rows.reshape(-1, MODEL_WIDTH).astype(jnp.float32) + gain_vector * projected_rows + control_residual.astype(jnp.float32)
        return final_output.astype(jnp.bfloat16).reshape(PATCH_ROWS, PATCH_COLUMNS, MODEL_WIDTH)
    return lax.map(single_image, (control_hidden_state, patch_segment_labels, patch_depth_levels, timestep_gain, transformer_hidden_state, query, key, value))
```

```python
import functools
import math

import jax
import jax.numpy as jnp
from jax import lax
from jax.experimental import pallas as pl
from jax.experimental.pallas import tpu as pltpu
from jax.sharding import PartitionSpec as P

HEAD_DIM = 128
MESH = pl.DeviceIdType.MESH
F32 = jnp.float32
BF16 = jnp.bfloat16


def time_embed(timestep, timestep_weight):
    half = timestep_weight.shape[0] // 2
    freqs = jnp.exp(-math.log(10000.0) * jnp.arange(half, dtype=F32) / half)
    angles = timestep.astype(F32)[:, None] * freqs[None, :]
    features = jnp.concatenate([jnp.cos(angles), jnp.sin(angles)], axis=1).astype(BF16)
    return jax.nn.silu(jnp.dot(features, timestep_weight, preferred_element_type=F32))


def condition_kernel(depth_base, x_ref, seg_ref, dep_ref, table_ref, gain_ref, o_ref, rows_ref):
    grid_rows, grid_cols = x_ref.shape[1], x_ref.shape[2]
    for r in range(grid_rows):
        rows_ref[r * grid_cols : (r + 1) * grid_cols, :] = x_ref[0, r].astype(F32)
    tokens, classes = rows_ref.shape[0], table_ref.shape[0]
    iota = lax.broadcasted_iota(jnp.int32, (tokens, classes), 1)
    hit = jnp.logical_or(iota == seg_ref[0], iota == dep_ref[0] + depth_base)
    onehot = jnp.where(hit, 1.0, 0.0).astype(BF16)
    mixed = rows_ref[...] + jnp.dot(onehot, table_ref[...], preferred_element_type=F32)
    scale = lax.rsqrt(jnp.mean(mixed * mixed, axis=-1, keepdims=True) + 1e-06)
    o_ref[0] = (mixed * scale * gain_ref[0]).astype(BF16)


def condition(hidden, seg, dep, seg_table, dep_table, gain_rows, groups):
    images, rows, cols, width = hidden.shape
    part = rows // groups
    tokens = part * cols
    depth_base = -(-seg_table.shape[0] // 256) * 256
    table = jnp.concatenate(
        [jnp.pad(seg_table, ((0, depth_base - seg_table.shape[0]), (0, 0))), dep_table], axis=0
    )
    column = pl.BlockSpec((1, tokens, 1), lambda b, r: (b, r, 0))
    return pl.pallas_call(
        functools.partial(condition_kernel, depth_base),
        out_shape=jax.ShapeDtypeStruct((images, rows * cols, width), BF16),
        grid=(images, groups),
        in_specs=[
            pl.BlockSpec((1, part, cols, width), lambda b, r: (b, r, 0, 0)),
            column,
            column,
            pl.BlockSpec(table.shape, lambda b, r: (0, 0)),
            pl.BlockSpec((1, 1, width), lambda b, r: (b, 0, 0)),
        ],
        out_specs=pl.BlockSpec((1, tokens, width), lambda b, r: (b, r, 0)),
        scratch_shapes=[pltpu.VMEM((tokens, width), F32)],
        compiler_params=pltpu.CompilerParams(vmem_limit_bytes=48 * 2**20),
    )(
        hidden,
        seg.reshape(images, rows * cols, 1),
        dep.reshape(images, rows * cols, 1),
        table,
        gain_rows[:, None, :],
    )


def exchange_kernel(
    n_ctl, n_seq,
    q_ref, k_ref, v_ref, c_ref, wc_ref, wa_ref,
    att_ref, c1_ref, c2_ref, wcf_ref, waf_ref,
    qb, kb, vb, vx, ob,
    qkv_s, qkv_r, o_s, o_r, c1_s, c1_r, c2_s, c2_r,
    wz_s, wz_r, wp_s, wp_r, wf_s, wf_r, az_s, az_r, af_s, af_r, loc,
):
    z, s = lax.axis_index("ctl"), lax.axis_index("seq")
    core = lax.rem(s, 2)
    sib = s + 1 - 2 * core
    seq_peers = [lax.rem(s + i, n_seq) for i in range(1, n_seq)]
    ctl_peers = [lax.rem(z + i, n_ctl) for i in range(1, n_ctl)]

    barrier = pltpu.get_barrier_semaphore()
    for p in seq_peers:
        pl.semaphore_signal(barrier, inc=1, device_id=(z, p), device_id_type=MESH)
    for p in ctl_peers:
        pl.semaphore_signal(barrier, inc=1, device_id=(p, s), device_id_type=MESH)
    pl.semaphore_wait(barrier, n_seq + n_ctl - 2)

    images, own_tokens, inner = q_ref.shape
    length = own_tokens * n_seq
    hw = inner // n_seq
    heads = hw // HEAD_DIM

    def rem(src, dst, ss, rs, dz, ds):
        return pltpu.make_async_remote_copy(
            src_ref=src, dst_ref=dst, send_sem=ss, recv_sem=rs,
            device_id=(dz, ds), device_id_type=MESH,
        )

    def aligned(i, n):
        return pl.ds(pl.multiple_of(i * n, n), n)

    wc_rows = wc_ref.shape[0] // n_seq
    wc_mine = wc_ref.at[aligned(s, wc_rows)]
    wa_half = wa_ref.shape[0] // 2
    wa_mine = wa_ref.at[aligned(core, wa_half)]

    wz = [rem(wc_mine, wcf_ref.at[z, s], wz_s.at[i], wz_r.at[i], p, s) for i, p in enumerate(ctl_peers)]
    az = [rem(wa_mine, waf_ref.at[z, core], az_s.at[i], az_r.at[i], p, s) for i, p in enumerate(ctl_peers)]

    own_images, ctl_rows, _ = c_ref.shape
    ct = ctl_rows // n_seq
    c1 = [
        rem(c_ref.at[:, aligned(p, ct), :], c1_ref.at[pl.ds(s * own_images, own_images)],
            c1_s.at[i], c1_r.at[i], z, p)
        for i, p in enumerate(seq_peers)
    ]
    qkv = [
        [
            rem(src.at[g, :, aligned(p, hw)], dst.at[g, aligned(s, own_tokens), :],
                qkv_s.at[g, a, i], qkv_r.at[g, a, i], z, p)
            for a, (src, dst) in enumerate(((q_ref, qb), (k_ref, kb), (v_ref, vb)))
            for i, p in enumerate(seq_peers)
        ]
        for g in range(images)
    ]
    local = [
        pltpu.make_async_copy(wc_mine, wcf_ref.at[z, s], loc.at[0]),
        pltpu.make_async_copy(wa_ref.at[aligned(0, wa_half)], waf_ref.at[z, 0], loc.at[1]),
        pltpu.make_async_copy(wa_ref.at[aligned(1, wa_half)], waf_ref.at[z, 1], loc.at[2]),
        pltpu.make_async_copy(
            c_ref.at[:, aligned(s, ct), :], c1_ref.at[pl.ds(s * own_images, own_images)], loc.at[3]),
    ]
    mine = [
        pltpu.make_async_copy(
            src.at[g, :, aligned(s, hw)], dst.at[g, aligned(s, own_tokens), :], loc.at[4 + 3 * g + a])
        for g in range(images)
        for a, (src, dst) in enumerate(((q_ref, qb), (k_ref, kb), (v_ref, vb)))
    ]

    for c in wz + c1 + qkv[0]:
        c.start()
    for c in local + mine:
        c.start()
    for g in range(1, images):
        for c in qkv[g]:
            c.start()
    for c in az:
        c.start()

    for c in c1:
        c.wait_recv()
    local[3].wait()
    pair = c1_ref.shape[0] // n_ctl
    c2 = [
        rem(c1_ref.at[pl.ds(p * pair, pair)], c2_ref.at[z], c2_s.at[i], c2_r.at[i], p, s)
        for i, p in enumerate(ctl_peers)
    ]
    for c in c2:
        c.start()
    c2_own = pltpu.make_async_copy(
        c1_ref.at[pl.ds(z * pair, pair)], c2_ref.at[z], loc.at[4 + 3 * images])
    c2_own.start()

    for c in wz:
        c.wait_recv()
    local[0].wait()
    chip_peers = [lax.rem(s + 2 * j, n_seq) for j in range(1, n_seq // 2)]
    wp = [
        rem(wcf_ref.at[:, s], wcf_ref.at[:, s], wp_s.at[i], wp_r.at[i], z, p)
        for i, p in enumerate(chip_peers)
    ]
    for c in wp:
        c.start()
    wf = [rem(wcf_ref.at[:, s], wcf_ref.at[:, s], wf_s.at[0], wf_r.at[0], z, sib)]
    wf[0].start()

    scale = HEAD_DIM ** (-0.5) * math.log2(math.e)
    block = math.gcd(length, 256)
    o_copies = []
    for g in range(images):
        for c in qkv[g]:
            c.wait_recv()
        for a in range(3):
            mine[3 * g + a].wait()
        for h in range(heads):
            vx[h, :, 0:HEAD_DIM] = vb[g, :, h * HEAD_DIM : (h + 1) * HEAD_DIM]
            if g == 0:
                vx[h, :, HEAD_DIM : 2 * HEAD_DIM] = jnp.ones((length, HEAD_DIM), BF16)

        @pl.loop(0, length // block)
        def _(j):
            rows = pl.ds(pl.multiple_of(j * block, block), block)
            for h in range(heads):
                cols = slice(h * HEAD_DIM, (h + 1) * HEAD_DIM)
                scores = lax.dot_general(
                    qb[g, rows, cols], kb[g, :, cols], (((1,), (1,)), ((), ())),
                    preferred_element_type=F32,
                )
                peak = jnp.max(scores, axis=1, keepdims=True)
                weights = jnp.exp2((scores - peak) * scale).astype(BF16)
                mixed = jnp.dot(weights, vx[h], preferred_element_type=F32)
                ob[g, rows, cols] = (mixed[:, :HEAD_DIM] / mixed[:, HEAD_DIM:]).astype(BF16)

        for i, p in enumerate(seq_peers):
            c = rem(ob.at[g, aligned(p, own_tokens), :], att_ref.at[g, :, aligned(s, hw)],
                    o_s.at[g, i], o_r.at[g, i], z, p)
            c.start()
            o_copies.append(c)
        c = pltpu.make_async_copy(
            ob.at[g, aligned(s, own_tokens), :], att_ref.at[g, :, aligned(s, hw)],
            loc.at[5 + 3 * images + g])
        c.start()
        mine.append(c)

    for j in range(1, n_seq // 2):
        wp[j - 1].wait_recv()
        origin = lax.rem(s + n_seq - 2 * j, n_seq)
        c = rem(wcf_ref.at[:, origin], wcf_ref.at[:, origin], wf_s.at[j], wf_r.at[j], z, sib)
        c.start()
        wf.append(c)
    af = []
    for i in range(1, n_ctl):
        az[i - 1].wait_recv()
        origin = lax.rem(z + n_ctl - i, n_ctl)
        c = rem(waf_ref.at[origin, core], waf_ref.at[origin, core], af_s.at[i - 1], af_r.at[i - 1], z, sib)
        c.start()
        af.append(c)

    for c in c2 + o_copies + wf + af:
        c.wait_recv()
    local[1].wait()
    local[2].wait()
    c2_own.wait()
    for c in mine[3 * images :]:
        c.wait()
    for c in wz + az + c1 + c2 + wp + wf + af + o_copies:
        c.wait_send()
    for g in range(images):
        for c in qkv[g]:
            c.wait_send()


def exchange(q, k, v, normed, wc, wa, n_ctl, n_seq):
    images, own_tokens, inner = q.shape
    length = own_tokens * n_seq
    hw = inner // n_seq
    own_images, ctl_rows, width = normed.shape
    ct = ctl_rows // n_seq
    total = own_images * n_seq
    dma = lambda *shape: pltpu.SemaphoreType.DMA(shape)
    anywhere = pl.BlockSpec(memory_space=pl.ANY)
    flops = 4 * images * length * length * hw
    return pl.pallas_call(
        functools.partial(exchange_kernel, n_ctl, n_seq),
        out_shape=[
            jax.ShapeDtypeStruct(q.shape, BF16),
            jax.ShapeDtypeStruct((total, ct, width), BF16),
            jax.ShapeDtypeStruct((n_ctl, total // n_ctl, ct, width), BF16),
            jax.ShapeDtypeStruct((n_ctl, n_seq, wc.shape[0] // n_seq, wc.shape[1]), BF16),
            jax.ShapeDtypeStruct((n_ctl, 2, wa.shape[0] // 2, wa.shape[1]), BF16),
        ],
        in_specs=[anywhere] * 6,
        out_specs=[anywhere] * 5,
        scratch_shapes=[
            pltpu.VMEM((images, length, hw), BF16),
            pltpu.VMEM((images, length, hw), BF16),
            pltpu.VMEM((images, length, hw), BF16),
            pltpu.VMEM((hw // HEAD_DIM, length, 2 * HEAD_DIM), BF16),
            pltpu.VMEM((images, length, hw), BF16),
            dma(images, 3, n_seq - 1), dma(images, 3, n_seq - 1),
            dma(images, n_seq - 1), dma(images, n_seq - 1),
            dma(n_seq - 1), dma(n_seq - 1),
            dma(n_ctl - 1), dma(n_ctl - 1),
            dma(n_ctl - 1), dma(n_ctl - 1),
            dma(n_seq // 2 - 1), dma(n_seq // 2 - 1),
            dma(n_seq // 2), dma(n_seq // 2),
            dma(n_ctl - 1), dma(n_ctl - 1),
            dma(n_ctl - 1), dma(n_ctl - 1),
            dma(5 + 4 * images),
        ],
        compiler_params=pltpu.CompilerParams(
            collective_id=0, has_side_effects=True, vmem_limit_bytes=52 * 2**20
        ),
        cost_estimate=pl.CostEstimate(
            flops=flops, bytes_accessed=64 * 2**20, transcendentals=images * length * length * 2
        ),
    )(q, k, v, normed, wc, wa)


def per_device(
    n_ctl, n_seq,
    control_hidden_state,
    patch_segment_labels,
    patch_depth_levels,
    timestep,
    segment_label_embedding,
    depth_level_embedding,
    timestep_weight,
    control_norm_gain,
    control_output_weight,
    transformer_hidden_state,
    query,
    key,
    value,
    attention_output_weight,
):
    gain = time_embed(timestep, timestep_weight)
    own_images, _, ctl_cols, width = control_hidden_state.shape
    ctl_gain = lax.dynamic_slice_in_dim(gain, lax.axis_index("seq") * own_images, own_images, 0)
    normed = condition(
        control_hidden_state,
        patch_segment_labels,
        patch_depth_levels,
        segment_label_embedding,
        depth_level_embedding,
        control_norm_gain * (1.0 + ctl_gain),
        n_seq,
    )
    images, rows, cols, inner = query.shape
    tokens = rows * cols
    flat = lambda a: a.reshape(images, tokens, inner)
    attended, _, arrived, wc_full, wa_full = exchange(
        flat(query), flat(key), flat(value), normed,
        control_output_weight, attention_output_weight, n_ctl, n_seq,
    )
    out_index = jnp.arange(images * tokens, dtype=jnp.int32)
    image, place = out_index // tokens, out_index % tokens
    row, col = place // cols, place % cols
    source = (
        ((col // ctl_cols) * images + image) * (rows * ctl_cols) + row * ctl_cols + col % ctl_cols
    )
    order = (source[:, None] == out_index[None, :]).astype(BF16)
    normed_rows = jnp.dot(
        order, arrived.reshape(images * tokens, width), preferred_element_type=F32
    ).astype(BF16)
    residual = jnp.dot(
        normed_rows, wc_full.reshape(-1, width), preferred_element_type=F32
    ).astype(BF16)
    projected = jnp.dot(
        attended.reshape(images * tokens, inner),
        wa_full.reshape(inner, width),
        preferred_element_type=F32,
    )
    t_gain = lax.dynamic_slice_in_dim(gain, lax.axis_index("ctl") * images, images, 0)
    shape = (images, tokens, width)
    final = (
        transformer_hidden_state.reshape(shape).astype(F32)
        + t_gain[:, None, :] * projected.reshape(shape)
        + residual.reshape(shape).astype(F32)
    )
    return final.astype(BF16).reshape(transformer_hidden_state.shape)


def solution(mesh):
    return jax.shard_map(
        functools.partial(per_device, mesh.shape["ctl"], mesh.shape["seq"]),
        mesh=mesh,
        in_specs=(
            P("seq", None, "ctl", None),
            P("seq", None, "ctl"),
            P("seq", None, "ctl"),
            P(),
            P(),
            P(),
            P(),
            P(),
            P("ctl", None),
            P("ctl", "seq", None, None),
            P("ctl", "seq", None, None),
            P("ctl", "seq", None, None),
            P("ctl", "seq", None, None),
            P("ctl", None),
        ),
        out_specs=P("ctl", "seq", None, None),
        check_vma=False,
    )
```

```python
import functools
import math

import jax
import jax.numpy as jnp
from jax import lax
from jax.experimental import pallas as pl
from jax.experimental.pallas import tpu as pltpu
from jax.sharding import PartitionSpec as P

HEAD_DIM = 128
MESH = pl.DeviceIdType.MESH
F32 = jnp.float32
BF16 = jnp.bfloat16


def time_embed(timestep, timestep_weight):
    half = timestep_weight.shape[0] // 2
    freqs = jnp.exp(-math.log(10000.0) * jnp.arange(half, dtype=F32) / half)
    angles = timestep.astype(F32)[:, None] * freqs[None, :]
    features = jnp.concatenate([jnp.cos(angles), jnp.sin(angles)], axis=1).astype(BF16)
    return jax.nn.silu(jnp.dot(features, timestep_weight, preferred_element_type=F32))


def exchange_kernel(
    n_ctl, n_seq, depth_base,
    q_ref, k_ref, v_ref, x_ref, wc_ref, wa_ref, seg_ref, dep_ref, table_ref, gain_ref, order_ref,
    att_ref, res_ref, c1_ref, wcf_ref, waf_ref,
    qb, kb, vb, vx, ob, xb, rows_f, nrm, xr, wb,
    qkv_s, qkv_r, o_s, o_r, c1_s, c1_r, c2_s, c2_r,
    wz_s, wz_r, wp_s, wp_r, wr_s, wr_r, wf_s, wf_r, az_s, az_r, af_s, af_r, loc, xs, ws,
):
    z, s = lax.axis_index("ctl"), lax.axis_index("seq")
    core = lax.rem(s, 2)
    sib = s + 1 - 2 * core
    seq_peers = [lax.rem(s + i, n_seq) for i in range(1, n_seq)]
    ctl_peers = [lax.rem(z + i, n_ctl) for i in range(1, n_ctl)]

    barrier = pltpu.get_barrier_semaphore()
    for p in seq_peers:
        pl.semaphore_signal(barrier, inc=1, device_id=(z, p), device_id_type=MESH)
    for p in ctl_peers:
        pl.semaphore_signal(barrier, inc=1, device_id=(p, s), device_id_type=MESH)
    pl.semaphore_wait(barrier, n_seq + n_ctl - 2)

    images, own_tokens, inner = q_ref.shape
    length = own_tokens * n_seq
    hw = inner // n_seq
    heads = hw // HEAD_DIM
    width = x_ref.shape[3]

    def rem(src, dst, ss, rs, dz, ds):
        return pltpu.make_async_remote_copy(
            src_ref=src, dst_ref=dst, send_sem=ss, recv_sem=rs,
            device_id=(dz, ds), device_id_type=MESH,
        )

    def aligned(i, n):
        return pl.ds(pl.multiple_of(i * n, n), n)

    wc_rows = wc_ref.shape[0] // n_seq
    wc_mine = wc_ref.at[aligned(s, wc_rows)]
    wa_half = wa_ref.shape[0] // 2
    wa_mine = wa_ref.at[aligned(core, wa_half)]
    wz = [rem(wc_mine, wcf_ref.at[z, s], wz_s.at[i], wz_r.at[i], p, s) for i, p in enumerate(ctl_peers)]

    def az(way, step, act):
        step_z = 1 - 2 * way
        origin = z - step_z * (step - 1)
        to = z + step_z
        source_ok = jnp.logical_and(origin >= 0, origin < n_ctl)
        ok = jnp.logical_and(source_ok, jnp.logical_and(to >= 0, to < n_ctl))

        @pl.when(ok)
        def _():
            src = wa_mine if step == 1 else waf_ref.at[origin, core]
            c = rem(src, waf_ref.at[origin, core], az_s.at[way, step - 1], az_r.at[way, step - 1], to, s)
            if act == "start":
                c.start()
            else:
                c.wait_send()

    def az_arrived(way, step, act):
        origin = z - (1 - 2 * way) * step

        @pl.when(jnp.logical_and(origin >= 0, origin < n_ctl))
        def _():
            ref = waf_ref.at[origin, core]
            if act == "wait":
                rem(ref, ref, az_s.at[way, step - 1], az_r.at[way, step - 1], z, sib).wait_recv()
                return
            c = rem(ref, ref, af_s.at[way, step - 1], af_r.at[way, step - 1], z, sib)
            if act == "pass":
                c.start()
            elif act == "passed":
                c.wait_recv()
            else:
                c.wait_send()

    def both(f, step, act):
        for way in range(2):
            f(way, step, act)

    qkv = [
        [
            rem(src.at[g, :, aligned(p, hw)], dst.at[g, aligned(s, own_tokens), :],
                qkv_s.at[g, a, i], qkv_r.at[g, a, i], z, p)
            for a, (src, dst) in enumerate(((q_ref, qb), (k_ref, kb), (v_ref, vb)))
            for i, p in enumerate(seq_peers)
        ]
        for g in range(images)
    ]
    local = [
        pltpu.make_async_copy(wc_mine, wcf_ref.at[z, s], loc.at[0]),
        pltpu.make_async_copy(wa_ref.at[aligned(0, wa_half)], waf_ref.at[z, 0], loc.at[1]),
        pltpu.make_async_copy(wa_ref.at[aligned(1, wa_half)], waf_ref.at[z, 1], loc.at[2]),
    ]
    mine = [
        pltpu.make_async_copy(
            src.at[g, :, aligned(s, hw)], dst.at[g, aligned(s, own_tokens), :], loc.at[4 + 3 * g + a])
        for g in range(images)
        for a, (src, dst) in enumerate(((q_ref, qb), (k_ref, kb), (v_ref, vb)))
    ]

    for c in wz + qkv[0]:
        c.start()
    both(az, 1, "start")

    own_images, grid_rows, grid_cols = x_ref.shape[0], x_ref.shape[1], x_ref.shape[2]
    part = grid_rows // n_seq
    ct = part * grid_cols
    groups = own_images * n_seq

    def x_copy(t, slot):
        return pltpu.make_async_copy(
            x_ref.at[t // n_seq, pl.ds(lax.rem(t, n_seq) * part, part)], xb.at[slot], xs.at[slot])

    x_copy(0, 0).start()
    for c in local + mine:
        c.start()

    @pl.loop(0, groups)
    def _(t):
        slot = lax.rem(t, 2)

        @pl.when(t + 1 < groups)
        def _():
            x_copy(t + 1, 1 - slot).start()

        x_copy(t, slot).wait()
        for r in range(part):
            rows_f[r * grid_cols : (r + 1) * grid_cols, :] = xb[slot, r].astype(F32)
        iota = lax.broadcasted_iota(jnp.int32, (ct, table_ref.shape[0]), 1)
        hit = jnp.logical_or(iota == seg_ref[t], iota == dep_ref[t] + depth_base)
        onehot = jnp.where(hit, 1.0, 0.0).astype(BF16)
        mixed = rows_f[...] + jnp.dot(onehot, table_ref[...], preferred_element_type=F32)
        norm = lax.rsqrt(jnp.mean(mixed * mixed, axis=-1, keepdims=True) + 1e-06)
        nrm[t] = (mixed * norm * gain_ref[t // n_seq]).astype(BF16)

    c1 = [
        [
            rem(nrm.at[b * n_seq + p], c1_ref.at[s * own_images + b], c1_s.at[b, i], c1_r.at[b, i], z, p)
            for i, p in enumerate(seq_peers)
        ]
        for b in range(own_images)
    ]
    c1 = [c for each in c1 for c in each]
    c1_own = [
        pltpu.make_async_copy(nrm.at[b * n_seq + s], c1_ref.at[s * own_images + b], loc.at[5 + 4 * images + b])
        for b in range(own_images)
    ]
    for c in c1 + c1_own:
        c.start()
    for g in range(1, images):
        for c in qkv[g]:
            c.start()

    scale = HEAD_DIM ** (-0.5) * math.log2(math.e)
    block = math.gcd(length, 256)
    o_copies = []
    o_mine = []

    def attend(g):
        for c in qkv[g]:
            c.wait_recv()
        for a in range(3):
            mine[3 * g + a].wait()
        for h in range(heads):
            vx[h, :, 0:HEAD_DIM] = vb[g, :, h * HEAD_DIM : (h + 1) * HEAD_DIM]
            if g == 0:
                vx[h, :, HEAD_DIM : 2 * HEAD_DIM] = jnp.ones((length, HEAD_DIM), BF16)

        @pl.loop(0, length // block)
        def _(j):
            rows = pl.ds(pl.multiple_of(j * block, block), block)
            for h in range(heads):
                cols = slice(h * HEAD_DIM, (h + 1) * HEAD_DIM)
                scores = lax.dot_general(
                    qb[g, rows, cols], kb[g, :, cols], (((1,), (1,)), ((), ())),
                    preferred_element_type=F32,
                )
                peak = jnp.max(scores, axis=1, keepdims=True)
                weights = jnp.exp2((scores - peak) * scale).astype(BF16)
                mixed = jnp.dot(weights, vx[h], preferred_element_type=F32)
                ob[g, rows, cols] = (mixed[:, :HEAD_DIM] / mixed[:, HEAD_DIM:]).astype(BF16)

        for i, p in enumerate(seq_peers):
            c = rem(ob.at[g, aligned(p, own_tokens), :], att_ref.at[g, :, aligned(s, hw)],
                    o_s.at[g, i], o_r.at[g, i], z, p)
            c.start()
            o_copies.append(c)
        c = pltpu.make_async_copy(
            ob.at[g, aligned(s, own_tokens), :], att_ref.at[g, :, aligned(s, hw)],
            loc.at[5 + 3 * images + g])
        c.start()
        o_mine.append(c)

    attend(0)

    for c in wz:
        c.wait_recv()
    local[0].wait()

    def rows_to(first, last, origin, ss, rs, to):
        ref = wcf_ref.at[first:last, origin]
        return rem(ref, ref, ss, rs, z, to)

    relayed = n_seq == 8
    if relayed:
        side = s + 2 - 4 * lax.rem(s // 2, 2)
        across = s + 4 - 8 * (s // 4)
        chip_peers = [side, across]
        origins = [side, across, side + across - s]
    else:
        chip_peers = [lax.rem(s + 2 * j, n_seq) for j in range(1, n_seq // 2)]
        origins = [lax.rem(s + n_seq - 2 * j, n_seq) for j in range(1, n_seq // 2)]
    wp = [rows_to(0, n_ctl, s, wp_s.at[i], wp_r.at[i], p) for i, p in enumerate(chip_peers)]
    for c in wp:
        c.start()
    wf = [rows_to(0, n_ctl, s, wf_s.at[0], wf_r.at[0], sib)]
    wf[0].start()

    for c in c1:
        c.wait_recv()
    for c in c1_own:
        c.wait()
    pair = c1_ref.shape[0] // n_ctl
    c2 = [
        rem(c1_ref.at[pl.ds(p * pair, pair)], xr.at[z], c2_s.at[i], c2_r.at[i], p, s)
        for i, p in enumerate(ctl_peers)
    ]
    for c in c2:
        c.start()
    c2_own = pltpu.make_async_copy(
        c1_ref.at[pl.ds(z * pair, pair)], xr.at[z], loc.at[4 + 3 * images])
    c2_own.start()
    both(az_arrived, 1, "wait")
    local[1].wait()
    local[2].wait()
    if n_ctl > 2:
        both(az, 2, "start")

    for g in range(1, images):
        attend(g)

    wr = []
    half = n_ctl // 2
    for i, c in enumerate(wp):
        c.wait_recv()
        if relayed:
            first, last = ((0, half), (half, n_ctl))[i]
            c = rows_to(first, last, chip_peers[i], wr_s.at[i], wr_r.at[i], chip_peers[1 - i])
            c.start()
            wr.append(c)
    for i in range(len(wp)):
        c = rows_to(0, n_ctl, origins[i], wf_s.at[i + 1], wf_r.at[i + 1], sib)
        c.start()
        wf.append(c)
    both(az_arrived, 1, "pass")
    for step in range(2, n_ctl):
        both(az_arrived, step, "wait")
        if step + 1 < n_ctl:
            both(az, step + 1, "start")
        both(az_arrived, step, "pass")
    for c in wr:
        c.wait_recv()
    if relayed:
        c = rows_to(0, n_ctl, origins[2], wf_s.at[3], wf_r.at[3], sib)
        c.start()
        wf.append(c)

    for c in c2:
        c.wait_recv()
    c2_own.wait()
    for c in c1:
        c.wait_send()
    tile = wb.shape[4]
    tokens = nrm.shape[0] * nrm.shape[1]

    @pl.loop(0, width // tile)
    def _(j):
        cols = aligned(j, tile)
        x = xr[:, :, :, cols].reshape(tokens, tile)
        y = jnp.dot(order_ref[...], x, preferred_element_type=F32)
        nrm[:, :, cols] = y.astype(BF16).reshape(nrm.shape[0], nrm.shape[1], tile)

    for c in wf:
        c.wait_recv()

    def w_copy(j, slot):
        return pltpu.make_async_copy(
            wcf_ref.at[:, :, :, aligned(j, tile)], wb.at[slot], ws.at[slot])

    w_copy(0, 0).start()

    @pl.loop(0, width // tile)
    def _(j):
        slot = lax.rem(j, 2)

        @pl.when(j + 1 < width // tile)
        def _():
            w_copy(j + 1, 1 - slot).start()

        w_copy(j, slot).wait()
        y = jnp.dot(
            nrm[...].reshape(tokens, width), wb[slot].reshape(width, tile),
            preferred_element_type=F32,
        )
        xr[:, :, :, aligned(j, tile)] = y.astype(BF16).reshape(xr.shape[:3] + (tile,))

    done = pltpu.make_async_copy(xr, res_ref, loc.at[3])
    done.start()

    for c in o_copies:
        c.wait_recv()
    for c in o_mine:
        c.wait()
    for step in range(1, n_ctl):
        both(az_arrived, step, "passed")
        both(az_arrived, step, "sent")
        both(az, step, "sent")
    for c in wz + c2 + wp + wr + wf + o_copies:
        c.wait_send()
    for g in range(images):
        for c in qkv[g]:
            c.wait_send()
    done.wait()


def exchange(q, k, v, hidden, wc, wa, seg, dep, table, depth_base, gain_rows, order, n_ctl, n_seq):
    images, own_tokens, inner = q.shape
    length = own_tokens * n_seq
    hw = inner // n_seq
    own_images, grid_rows, grid_cols, width = hidden.shape
    part = grid_rows // n_seq
    ct = part * grid_cols
    total = own_images * n_seq
    pair = total // n_ctl
    tile = math.gcd(width, 256)
    wc_rows = wc.shape[0] // n_seq
    dma = lambda *shape: pltpu.SemaphoreType.DMA(shape)
    anywhere = pl.BlockSpec(memory_space=pl.ANY)
    held = pl.BlockSpec(memory_space=pltpu.VMEM)
    flops = 4 * images * length * length * hw
    return pl.pallas_call(
        functools.partial(exchange_kernel, n_ctl, n_seq, depth_base),
        out_shape=[
            jax.ShapeDtypeStruct(q.shape, BF16),
            jax.ShapeDtypeStruct((n_ctl, pair, ct, width), BF16),
            jax.ShapeDtypeStruct((total, ct, width), BF16),
            jax.ShapeDtypeStruct((n_ctl, n_seq, wc_rows, width), BF16),
            jax.ShapeDtypeStruct((n_ctl, 2, wa.shape[0] // 2, wa.shape[1]), BF16),
        ],
        in_specs=[anywhere] * 6 + [held] * 5,
        out_specs=[anywhere] * 5,
        scratch_shapes=[
            pltpu.VMEM((images, length, hw), BF16),
            pltpu.VMEM((images, length, hw), BF16),
            pltpu.VMEM((images, length, hw), BF16),
            pltpu.VMEM((hw // HEAD_DIM, length, 2 * HEAD_DIM), BF16),
            pltpu.VMEM((images, length, hw), BF16),
            pltpu.VMEM((2, part, grid_cols, width), BF16),
            pltpu.VMEM((ct, width), F32),
            pltpu.VMEM((total, ct, width), BF16),
            pltpu.VMEM((n_ctl, pair, ct, width), BF16),
            pltpu.VMEM((2, n_ctl, n_seq, wc_rows, tile), BF16),
            dma(images, 3, n_seq - 1), dma(images, 3, n_seq - 1),
            dma(images, n_seq - 1), dma(images, n_seq - 1),
            dma(own_images, n_seq - 1), dma(own_images, n_seq - 1),
            dma(n_ctl - 1), dma(n_ctl - 1),
            dma(n_ctl - 1), dma(n_ctl - 1),
            dma(n_seq // 2), dma(n_seq // 2),
            dma(2), dma(2),
            dma(n_seq // 2), dma(n_seq // 2),
            dma(2, n_ctl - 1), dma(2, n_ctl - 1),
            dma(2, n_ctl - 1), dma(2, n_ctl - 1),
            dma(5 + 4 * images + own_images),
            dma(2),
            dma(2),
        ],
        compiler_params=pltpu.CompilerParams(
            collective_id=0, has_side_effects=True, vmem_limit_bytes=56 * 2**20
        ),
        cost_estimate=pl.CostEstimate(
            flops=flops, bytes_accessed=64 * 2**20, transcendentals=images * length * length * 2
        ),
    )(
        q, k, v, hidden, wc, wa,
        seg.reshape(total, ct, 1), dep.reshape(total, ct, 1), table, gain_rows[:, None, :], order,
    )


def per_device(
    n_ctl, n_seq,
    control_hidden_state,
    patch_segment_labels,
    patch_depth_levels,
    timestep,
    segment_label_embedding,
    depth_level_embedding,
    timestep_weight,
    control_norm_gain,
    control_output_weight,
    transformer_hidden_state,
    query,
    key,
    value,
    attention_output_weight,
):
    gain = time_embed(timestep, timestep_weight)
    own_images, _, ctl_cols, width = control_hidden_state.shape
    ctl_gain = lax.dynamic_slice_in_dim(gain, lax.axis_index("seq") * own_images, own_images, 0)
    images, rows, cols, inner = query.shape
    tokens = rows * cols
    flat = lambda a: a.reshape(images, tokens, inner)
    out_index = jnp.arange(images * tokens, dtype=jnp.int32)
    image, place = out_index // tokens, out_index % tokens
    row, col = place // cols, place % cols
    source = (
        ((col // ctl_cols) * images + image) * (rows * ctl_cols) + row * ctl_cols + col % ctl_cols
    )
    order = (source[:, None] == out_index[None, :]).astype(BF16)
    depth_base = -(-segment_label_embedding.shape[0] // 256) * 256
    table = jnp.concatenate(
        [
            jnp.pad(
                segment_label_embedding,
                ((0, depth_base - segment_label_embedding.shape[0]), (0, 0)),
            ),
            depth_level_embedding,
        ],
        axis=0,
    )
    attended, residual, _, _, wa_full = exchange(
        flat(query), flat(key), flat(value), control_hidden_state,
        control_output_weight, attention_output_weight,
        patch_segment_labels, patch_depth_levels, table, depth_base,
        control_norm_gain * (1.0 + ctl_gain), order, n_ctl, n_seq,
    )
    projected = jnp.dot(
        attended.reshape(images * tokens, inner),
        wa_full.reshape(inner, width),
        preferred_element_type=F32,
    )
    t_gain = lax.dynamic_slice_in_dim(gain, lax.axis_index("ctl") * images, images, 0)
    shape = (images, tokens, width)
    final = (
        transformer_hidden_state.reshape(shape).astype(F32)
        + t_gain[:, None, :] * projected.reshape(shape)
        + residual.reshape(shape).astype(F32)
    )
    return final.astype(BF16).reshape(transformer_hidden_state.shape)


def solution(mesh):
    return jax.shard_map(
        functools.partial(per_device, mesh.shape["ctl"], mesh.shape["seq"]),
        mesh=mesh,
        in_specs=(
            P("seq", None, "ctl", None),
            P("seq", None, "ctl"),
            P("seq", None, "ctl"),
            P(),
            P(),
            P(),
            P(),
            P(),
            P("ctl", None),
            P("ctl", "seq", None, None),
            P("ctl", "seq", None, None),
            P("ctl", "seq", None, None),
            P("ctl", "seq", None, None),
            P("ctl", None),
        ),
        out_specs=P("ctl", "seq", None, None),
        check_vma=False,
    )
```

```python
import functools
import math

import jax
import jax.numpy as jnp
from jax import lax
from jax.experimental import pallas as pl
from jax.experimental.pallas import tpu as pltpu
from jax.sharding import PartitionSpec as P

HEAD_DIM = 128
MESH = pl.DeviceIdType.MESH
F32 = jnp.float32
BF16 = jnp.bfloat16


def time_embed(timestep, timestep_weight):
    half = timestep_weight.shape[0] // 2
    freqs = jnp.exp(-math.log(10000.0) * jnp.arange(half, dtype=F32) / half)
    angles = timestep.astype(F32)[:, None] * freqs[None, :]
    features = jnp.concatenate([jnp.cos(angles), jnp.sin(angles)], axis=1).astype(BF16)
    return jax.nn.silu(jnp.dot(features, timestep_weight, preferred_element_type=F32))


def exchange_kernel(
    n_ctl, n_seq, depth_base,
    q_ref, k_ref, v_ref, x_ref, wc_ref, wa_ref, seg_ref, dep_ref, table_ref, gain_ref, order_ref,
    att_ref, res_ref, c1_ref, wcf_ref, waf_ref,
    qb, kb, vb, vx, ob, xb, rows_f, nrm, xr, wb,
    qkv_s, qkv_r, o_s, o_r, c1_s, c1_r, c2_s, c2_r,
    wz_s, wz_r, wp_s, wp_r, wr_s, wr_r, wf_s, wf_r, az_s, az_r, af_s, af_r, loc, xs, ws,
):
    z, s = lax.axis_index("ctl"), lax.axis_index("seq")
    core = lax.rem(s, 2)
    sib = s + 1 - 2 * core
    seq_peers = [lax.rem(s + i, n_seq) for i in range(1, n_seq)]
    ctl_peers = [lax.rem(z + i, n_ctl) for i in range(1, n_ctl)]

    barrier = pltpu.get_barrier_semaphore()
    for p in seq_peers:
        pl.semaphore_signal(barrier, inc=1, device_id=(z, p), device_id_type=MESH)
    for p in ctl_peers:
        pl.semaphore_signal(barrier, inc=1, device_id=(p, s), device_id_type=MESH)
    pl.semaphore_wait(barrier, n_seq + n_ctl - 2)

    images, own_tokens, inner = q_ref.shape
    length = own_tokens * n_seq
    hw = inner // n_seq
    heads = hw // HEAD_DIM
    width = x_ref.shape[3]

    def rem(src, dst, ss, rs, dz, ds):
        return pltpu.make_async_remote_copy(
            src_ref=src, dst_ref=dst, send_sem=ss, recv_sem=rs,
            device_id=(dz, ds), device_id_type=MESH,
        )

    def aligned(i, n):
        return pl.ds(pl.multiple_of(i * n, n), n)

    wc_rows = wc_ref.shape[0] // n_seq
    wc_mine = wc_ref.at[aligned(s, wc_rows)]
    wa_half = wa_ref.shape[0] // 2
    wa_mine = wa_ref.at[aligned(core, wa_half)]
    wz = [rem(wc_mine, wcf_ref.at[z, s], wz_s.at[i], wz_r.at[i], p, s) for i, p in enumerate(ctl_peers)]

    def az(way, step, act):
        step_z = 1 - 2 * way
        origin = z - step_z * (step - 1)
        to = z + step_z
        source_ok = jnp.logical_and(origin >= 0, origin < n_ctl)
        ok = jnp.logical_and(source_ok, jnp.logical_and(to >= 0, to < n_ctl))

        @pl.when(ok)
        def _():
            src = wa_mine if step == 1 else waf_ref.at[origin, core]
            c = rem(src, waf_ref.at[origin, core], az_s.at[way, step - 1], az_r.at[way, step - 1], to, s)
            if act == "start":
                c.start()
            else:
                c.wait_send()

    def az_arrived(way, step, act):
        origin = z - (1 - 2 * way) * step

        @pl.when(jnp.logical_and(origin >= 0, origin < n_ctl))
        def _():
            ref = waf_ref.at[origin, core]
            if act == "wait":
                rem(ref, ref, az_s.at[way, step - 1], az_r.at[way, step - 1], z, sib).wait_recv()
                return
            c = rem(ref, ref, af_s.at[way, step - 1], af_r.at[way, step - 1], z, sib)
            if act == "pass":
                c.start()
            elif act == "passed":
                c.wait_recv()
            else:
                c.wait_send()

    def both(f, step, act):
        for way in range(2):
            f(way, step, act)

    qkv = [
        [
            rem(src.at[g, :, aligned(p, hw)], dst.at[g, aligned(s, own_tokens), :],
                qkv_s.at[g, a, i], qkv_r.at[g, a, i], z, p)
            for a, (src, dst) in enumerate(((q_ref, qb), (k_ref, kb), (v_ref, vb)))
            for i, p in enumerate(seq_peers)
        ]
        for g in range(images)
    ]
    local = [
        pltpu.make_async_copy(wc_mine, wcf_ref.at[z, s], loc.at[0]),
        pltpu.make_async_copy(wa_ref.at[aligned(0, wa_half)], waf_ref.at[z, 0], loc.at[1]),
        pltpu.make_async_copy(wa_ref.at[aligned(1, wa_half)], waf_ref.at[z, 1], loc.at[2]),
    ]
    mine = [
        pltpu.make_async_copy(
            src.at[g, :, aligned(s, hw)], dst.at[g, aligned(s, own_tokens), :], loc.at[4 + 3 * g + a])
        for g in range(images)
        for a, (src, dst) in enumerate(((q_ref, qb), (k_ref, kb), (v_ref, vb)))
    ]

    first_q = n_seq - 1
    for c in wz + qkv[0][:first_q]:
        c.start()
    both(az, 1, "start")

    own_images, grid_cols, grid_rows = x_ref.shape[0], x_ref.shape[1], x_ref.shape[2]
    part = grid_rows // n_seq
    ct = part * grid_cols
    halves = n_seq // 2
    groups = own_images * halves

    def x_copy(t, slot):
        return pltpu.make_async_copy(
            x_ref.at[t // halves, :, aligned(lax.rem(t, halves), 2 * part), :], xb.at[slot], xs.at[slot])

    x_copy(0, 0).start()
    for c in local + mine:
        c.start()

    @pl.loop(0, groups)
    def _(t):
        slot = lax.rem(t, 2)

        @pl.when(t + 1 < groups)
        def _():
            x_copy(t + 1, 1 - slot).start()

        x_copy(t, slot).wait()
        for c in range(grid_cols):
            both_rows = xb[slot, c].astype(F32)
            for u in range(2):
                rows_f[u, c * part : (c + 1) * part, :] = both_rows[u * part : (u + 1) * part]
        iota = lax.broadcasted_iota(jnp.int32, (ct, table_ref.shape[0]), 1)
        for u in range(2):
            g = 2 * t + u
            hit = jnp.logical_or(iota == seg_ref[g], iota == dep_ref[g] + depth_base)
            onehot = jnp.where(hit, 1.0, 0.0).astype(BF16)
            mixed = rows_f[u] + jnp.dot(onehot, table_ref[...], preferred_element_type=F32)
            norm = lax.rsqrt(jnp.mean(mixed * mixed, axis=-1, keepdims=True) + 1e-06)
            nrm[g] = (mixed * norm * gain_ref[t // halves]).astype(BF16)

    c1 = [
        [
            rem(nrm.at[b * n_seq + p], c1_ref.at[s * own_images + b], c1_s.at[b, i], c1_r.at[b, i], z, p)
            for i, p in enumerate(seq_peers)
        ]
        for b in range(own_images)
    ]
    c1 = [c for each in c1 for c in each]
    c1_own = [
        pltpu.make_async_copy(nrm.at[b * n_seq + s], c1_ref.at[s * own_images + b], loc.at[5 + 4 * images + b])
        for b in range(own_images)
    ]
    for c in c1 + c1_own + qkv[0][first_q:]:
        c.start()

    for c in c1:
        c.wait_recv()
    for c in c1_own:
        c.wait()
    pair = c1_ref.shape[0] // n_ctl
    c2 = [
        rem(c1_ref.at[pl.ds(p * pair, pair)], xr.at[z], c2_s.at[i], c2_r.at[i], p, s)
        for i, p in enumerate(ctl_peers)
    ]
    for c in c2:
        c.start()
    c2_own = pltpu.make_async_copy(
        c1_ref.at[pl.ds(z * pair, pair)], xr.at[z], loc.at[4 + 3 * images])
    c2_own.start()
    for g in range(1, images):
        for c in qkv[g]:
            c.start()
    both(az_arrived, 1, "wait")
    local[1].wait()
    local[2].wait()
    if n_ctl > 2:
        both(az, 2, "start")


    for c in wz:
        c.wait_recv()
    local[0].wait()

    def rows_to(first, last, origin, ss, rs, to):
        ref = wcf_ref.at[first:last, origin]
        return rem(ref, ref, ss, rs, z, to)

    relayed = n_seq == 8
    if relayed:
        side = s + 2 - 4 * lax.rem(s // 2, 2)
        across = s + 4 - 8 * (s // 4)
        chip_peers = [side, across]
        origins = [side, across, side + across - s]
    else:
        chip_peers = [lax.rem(s + 2 * j, n_seq) for j in range(1, n_seq // 2)]
        origins = [lax.rem(s + n_seq - 2 * j, n_seq) for j in range(1, n_seq // 2)]
    wp = [rows_to(0, n_ctl, s, wp_s.at[i], wp_r.at[i], p) for i, p in enumerate(chip_peers)]
    for c in wp:
        c.start()
    wf = [rows_to(0, n_ctl, s, wf_s.at[0], wf_r.at[0], sib)]
    wf[0].start()

    scale = HEAD_DIM ** (-0.5) * math.log2(math.e)
    block = math.gcd(length, 256)
    o_copies = []
    o_mine = []

    def attend(g):
        for c in qkv[g]:
            c.wait_recv()
        for a in range(3):
            mine[3 * g + a].wait()
        for h in range(heads):
            vx[h, :, 0:HEAD_DIM] = vb[g, :, h * HEAD_DIM : (h + 1) * HEAD_DIM]
            if g == 0:
                vx[h, :, HEAD_DIM : 2 * HEAD_DIM] = jnp.ones((length, HEAD_DIM), BF16)

        @pl.loop(0, length // block)
        def _(j):
            rows = pl.ds(pl.multiple_of(j * block, block), block)
            for h in range(heads):
                cols = slice(h * HEAD_DIM, (h + 1) * HEAD_DIM)
                scores = lax.dot_general(
                    qb[g, rows, cols], kb[g, :, cols], (((1,), (1,)), ((), ())),
                    preferred_element_type=F32,
                )
                peak = jnp.max(scores, axis=1, keepdims=True)
                weights = jnp.exp2((scores - peak) * scale).astype(BF16)
                mixed = jnp.dot(weights, vx[h], preferred_element_type=F32)
                ob[g, rows, cols] = (mixed[:, :HEAD_DIM] / mixed[:, HEAD_DIM:]).astype(BF16)

        for i, p in enumerate(seq_peers):
            c = rem(ob.at[g, aligned(p, own_tokens), :], att_ref.at[g, :, aligned(s, hw)],
                    o_s.at[g, i], o_r.at[g, i], z, p)
            c.start()
            o_copies.append(c)
        c = pltpu.make_async_copy(
            ob.at[g, aligned(s, own_tokens), :], att_ref.at[g, :, aligned(s, hw)],
            loc.at[5 + 3 * images + g])
        c.start()
        o_mine.append(c)

    for g in range(images):
        attend(g)

    wr = []
    half = n_ctl // 2
    for i, c in enumerate(wp):
        c.wait_recv()
        if relayed:
            first, last = ((0, half), (half, n_ctl))[i]
            c = rows_to(first, last, chip_peers[i], wr_s.at[i], wr_r.at[i], chip_peers[1 - i])
            c.start()
            wr.append(c)
    for i in range(len(wp)):
        c = rows_to(0, n_ctl, origins[i], wf_s.at[i + 1], wf_r.at[i + 1], sib)
        c.start()
        wf.append(c)
    both(az_arrived, 1, "pass")
    for step in range(2, n_ctl - 1):
        both(az_arrived, step, "wait")
        both(az, step + 1, "start")
        both(az_arrived, step, "pass")
    for c in wr:
        c.wait_recv()
    if relayed:
        c = rows_to(0, n_ctl, origins[2], wf_s.at[3], wf_r.at[3], sib)
        c.start()
        wf.append(c)

    for c in c2:
        c.wait_recv()
    c2_own.wait()
    for c in c1:
        c.wait_send()
    tile = wb.shape[4]
    tokens = nrm.shape[0] * nrm.shape[1]

    @pl.loop(0, width // tile)
    def _(j):
        cols = aligned(j, tile)
        x = xr[:, :, :, cols].reshape(tokens, tile)
        y = jnp.dot(order_ref[...], x, preferred_element_type=F32)
        nrm[:, :, cols] = y.astype(BF16).reshape(nrm.shape[0], nrm.shape[1], tile)

    for c in wf:
        c.wait_recv()

    def w_copy(j, slot):
        return pltpu.make_async_copy(
            wcf_ref.at[:, :, :, aligned(j, tile)], wb.at[slot], ws.at[slot])

    w_copy(0, 0).start()

    @pl.loop(0, width // tile)
    def _(j):
        slot = lax.rem(j, 2)

        @pl.when(j + 1 < width // tile)
        def _():
            w_copy(j + 1, 1 - slot).start()

        w_copy(j, slot).wait()
        y = jnp.dot(
            nrm[...].reshape(tokens, width), wb[slot].reshape(width, tile),
            preferred_element_type=F32,
        )
        xr[:, :, :, aligned(j, tile)] = y.astype(BF16).reshape(xr.shape[:3] + (tile,))

    done = pltpu.make_async_copy(xr, res_ref, loc.at[3])
    done.start()

    if n_ctl > 2:
        both(az_arrived, n_ctl - 1, "wait")
        both(az_arrived, n_ctl - 1, "pass")

    for c in o_copies:
        c.wait_recv()
    for c in o_mine:
        c.wait()
    for step in range(1, n_ctl):
        both(az_arrived, step, "passed")
        both(az_arrived, step, "sent")
        both(az, step, "sent")
    for c in wz + c2 + wp + wr + wf + o_copies:
        c.wait_send()
    for g in range(images):
        for c in qkv[g]:
            c.wait_send()
    done.wait()


def exchange(q, k, v, hidden, wc, wa, seg, dep, table, depth_base, gain_rows, order, n_ctl, n_seq):
    images, own_tokens, inner = q.shape
    length = own_tokens * n_seq
    hw = inner // n_seq
    own_images, grid_rows, grid_cols, width = hidden.shape
    part = grid_rows // n_seq
    ct = part * grid_cols
    total = own_images * n_seq
    pair = total // n_ctl
    tile = math.gcd(width, 256)
    wc_rows = wc.shape[0] // n_seq
    dma = lambda *shape: pltpu.SemaphoreType.DMA(shape)
    anywhere = pl.BlockSpec(memory_space=pl.ANY)
    held = pl.BlockSpec(memory_space=pltpu.VMEM)
    flops = 4 * images * length * length * hw

    def by_column(labels):
        labels = labels.reshape(own_images, n_seq, part, grid_cols)
        return jnp.transpose(labels, (0, 1, 3, 2)).reshape(total, ct, 1)

    return pl.pallas_call(
        functools.partial(exchange_kernel, n_ctl, n_seq, depth_base),
        out_shape=[
            jax.ShapeDtypeStruct(q.shape, BF16),
            jax.ShapeDtypeStruct((n_ctl, pair, ct, width), BF16),
            jax.ShapeDtypeStruct((total, ct, width), BF16),
            jax.ShapeDtypeStruct((n_ctl, n_seq, wc_rows, width), BF16),
            jax.ShapeDtypeStruct((n_ctl, 2, wa.shape[0] // 2, wa.shape[1]), BF16),
        ],
        in_specs=[anywhere] * 6 + [held] * 5,
        out_specs=[anywhere] * 5,
        scratch_shapes=[
            pltpu.VMEM((images, length, hw), BF16),
            pltpu.VMEM((images, length, hw), BF16),
            pltpu.VMEM((images, length, hw), BF16),
            pltpu.VMEM((hw // HEAD_DIM, length, 2 * HEAD_DIM), BF16),
            pltpu.VMEM((images, length, hw), BF16),
            pltpu.VMEM((2, grid_cols, 2 * part, width), BF16),
            pltpu.VMEM((2, ct, width), F32),
            pltpu.VMEM((total, ct, width), BF16),
            pltpu.VMEM((n_ctl, pair, ct, width), BF16),
            pltpu.VMEM((2, n_ctl, n_seq, wc_rows, tile), BF16),
            dma(images, 3, n_seq - 1), dma(images, 3, n_seq - 1),
            dma(images, n_seq - 1), dma(images, n_seq - 1),
            dma(own_images, n_seq - 1), dma(own_images, n_seq - 1),
            dma(n_ctl - 1), dma(n_ctl - 1),
            dma(n_ctl - 1), dma(n_ctl - 1),
            dma(n_seq // 2), dma(n_seq // 2),
            dma(2), dma(2),
            dma(n_seq // 2), dma(n_seq // 2),
            dma(2, n_ctl - 1), dma(2, n_ctl - 1),
            dma(2, n_ctl - 1), dma(2, n_ctl - 1),
            dma(5 + 4 * images + own_images),
            dma(2),
            dma(2),
        ],
        compiler_params=pltpu.CompilerParams(
            collective_id=0, has_side_effects=True, vmem_limit_bytes=56 * 2**20
        ),
        cost_estimate=pl.CostEstimate(
            flops=flops, bytes_accessed=64 * 2**20, transcendentals=images * length * length * 2
        ),
    )(
        q, k, v, jnp.transpose(hidden, (0, 2, 1, 3)), wc, wa, by_column(seg), by_column(dep), table, gain_rows[:, None, :], order,
    )


def per_device(
    n_ctl, n_seq,
    control_hidden_state,
    patch_segment_labels,
    patch_depth_levels,
    timestep,
    segment_label_embedding,
    depth_level_embedding,
    timestep_weight,
    control_norm_gain,
    control_output_weight,
    transformer_hidden_state,
    query,
    key,
    value,
    attention_output_weight,
):
    gain = time_embed(timestep, timestep_weight)
    own_images, _, ctl_cols, width = control_hidden_state.shape
    ctl_gain = lax.dynamic_slice_in_dim(gain, lax.axis_index("seq") * own_images, own_images, 0)
    images, rows, cols, inner = query.shape
    tokens = rows * cols
    flat = lambda a: a.reshape(images, tokens, inner)
    out_index = jnp.arange(images * tokens, dtype=jnp.int32)
    image, place = out_index // tokens, out_index % tokens
    row, col = place // cols, place % cols
    source = (
        ((col // ctl_cols) * images + image) * (rows * ctl_cols) + (col % ctl_cols) * rows + row
    )
    order = (source[:, None] == out_index[None, :]).astype(BF16)
    depth_base = -(-segment_label_embedding.shape[0] // 256) * 256
    table = jnp.concatenate(
        [
            jnp.pad(
                segment_label_embedding,
                ((0, depth_base - segment_label_embedding.shape[0]), (0, 0)),
            ),
            depth_level_embedding,
        ],
        axis=0,
    )
    attended, residual, _, _, wa_full = exchange(
        flat(query), flat(key), flat(value), control_hidden_state,
        control_output_weight, attention_output_weight,
        patch_segment_labels, patch_depth_levels, table, depth_base,
        control_norm_gain * (1.0 + ctl_gain), order, n_ctl, n_seq,
    )
    projected = jnp.dot(
        attended.reshape(images * tokens, inner),
        wa_full.reshape(inner, width),
        preferred_element_type=F32,
    )
    t_gain = lax.dynamic_slice_in_dim(gain, lax.axis_index("ctl") * images, images, 0)
    shape = (images, tokens, width)
    final = (
        transformer_hidden_state.reshape(shape).astype(F32)
        + t_gain[:, None, :] * projected.reshape(shape)
        + residual.reshape(shape).astype(F32)
    )
    return final.astype(BF16).reshape(transformer_hidden_state.shape)


def solution(mesh):
    return jax.shard_map(
        functools.partial(per_device, mesh.shape["ctl"], mesh.shape["seq"]),
        mesh=mesh,
        in_specs=(
            P("seq", None, "ctl", None),
            P("seq", None, "ctl"),
            P("seq", None, "ctl"),
            P(),
            P(),
            P(),
            P(),
            P(),
            P("ctl", None),
            P("ctl", "seq", None, None),
            P("ctl", "seq", None, None),
            P("ctl", "seq", None, None),
            P("ctl", "seq", None, None),
            P("ctl", None),
        ),
        out_specs=P("ctl", "seq", None, None),
        check_vma=False,
    )
```
